128 devices in a mesh: mem: 16 (over x, z_lo, core), lev: 8 (over y, z_hi).
Axes of the slice: x: 4, y: 4, z: 4 (z_hi: 2, z_lo: 2; z = z_hi * 2 + z_lo), core: 2. Of those that a mesh axis runs over, the one named last changes fastest.
Arguments:
- control_vec: float32 [256, 64, 8192], P('mem', 'lev'), may hold values from -6 to 6
- ens_perturb: bfloat16 [256, 3, 64, 8192], P(None, None, 'lev', 'mem'), may hold values from -6 to 6
- loc_blocks: bfloat16 [64, 9, 128, 128], replicated, may hold values from -0.1875 to 0.1875
- tile_index: int32 [64, 9], replicated, may hold values from 0 to 63, all different within a row
- obs_weight: bfloat16 [3, 64, 256], P(None, 'lev'), may hold values from -0.4375 to 0.4375
- channel_level_mask: int32 [64, 256], P('lev'), may hold values 0 or 1
- obs_precision: float32 [256, 8192], P(None, 'mem'), may hold values from 2 to 64
Outputs:
- hess_vec: float32 [256, 64, 8192], P('mem', 'lev')
The draws below stay inside these ranges and needn't reach their ends.
Inputs may be any that keep to these rules, and one draw needn't show every extreme that they name: `tile_index`: each row names 9 different tiles; every tile is named by some row.
All inputs are finite; a program needn't handle non-finite values. No bound on the sum of `channel_level_mask` on one device may be relied on, other than what follows from the above.
Results may differ from the reference program's by a relative error of at most 0.012.
Values may be sent and summed in bfloat16 or wider, within the bound.
A program may use at most 192 MiB of HBM per device.

```python
import math
import jax
import jax.numpy as jnp
from jax import lax

TILE = 128
NEIGH = 9
VARS = 3
CHANNELS = 256
MEMBERS = 256
LEVELS = 64
POINTS = 8192
NTILES = 64


def place_ends(values, rng, low, top_value):
    longest = values.shape.index(max(values.shape))
    spots = []
    for shift in (0, 1):
        where = [jax.random.randint(jax.random.fold_in(rng, axis), (), 0, length) for axis, length in enumerate(values.shape)]
        where[longest] = (where[longest] + shift) % values.shape[longest]
        spots.append(tuple(where))
    return values.at[spots[0]].set(low).at[spots[1]].set(top_value)


def block_levels(stream_key, shape, cuts, least, top_value):
    loudness = 1.0
    for axis_at, blocks in cuts:
        heights = jax.random.uniform(jax.random.fold_in(jax.random.fold_in(stream_key, 6), axis_at), (blocks,), jnp.float32, least / len(cuts), top_value / len(cuts))
        loudness = loudness * jnp.repeat(jnp.exp(heights), shape[axis_at] // blocks).reshape((-1,) + (1,) * (len(shape) - 1 - axis_at))
    return loudness


def distinct(own_key, rows, number_of, top, lift):
    order = jax.random.permutation(jax.random.fold_in(own_key, 1), number_of)
    boost = order
    for power in range(3):
        boost = boost * boost // number_of
    boost = boost * lift // number_of
    lots = jax.random.randint(jax.random.fold_in(own_key, 2), (rows, number_of), 0, 4096) + boost
    sure = jax.random.permutation(jax.random.fold_in(own_key, 3), rows)[jnp.arange(number_of) % rows]
    lots = jnp.where(jnp.arange(rows)[:, None] == sure[None, :], 1 << 14, lots)
    merit = lots * number_of + jnp.arange(number_of)
    return lax.top_k(merit.astype(jnp.int32), top)[1].astype(jnp.int32)


def gaussian(key, extent, width, limit, cuts=(), dtype=jnp.bfloat16):
    array = width * jax.random.normal(key, extent, jnp.float32)
    if cuts:
        array = array * block_levels(key, extent, cuts, -0.22, 0.18)
    return jnp.clip(array, -limit, limit).astype(dtype)


def setup_inputs(seed: int = 0) -> dict:
    streams_of = jax.random.split(jax.random.key(seed), 8)
    return {
        "control_vec": gaussian(streams_of[0], (MEMBERS, LEVELS, POINTS), 1.0, 6.0, ((0, 16), (1, 8)), jnp.float32),
        "ens_perturb": gaussian(streams_of[1], (MEMBERS, VARS, LEVELS, POINTS), 1.0, 6.0, ((2, 8), (3, 16))),
        "loc_blocks": gaussian(streams_of[2], (NTILES, NEIGH, TILE, TILE), (NEIGH * TILE) ** -0.5, 0.1875),
        "tile_index": distinct(streams_of[3], NTILES, NTILES, NEIGH, 0),
        "obs_weight": gaussian(streams_of[4], (VARS, LEVELS, CHANNELS), (VARS * LEVELS) ** -0.5, 0.4375, ((1, 8),)),
        "channel_level_mask": place_ends((jax.random.randint(streams_of[5], (LEVELS, CHANNELS), 0, 2) < 1).astype(jnp.int32), jax.random.fold_in(streams_of[5], 1), 0, 1),
        "obs_precision": jnp.clip(jnp.exp(math.log(64.0) - 3.465736 * jax.random.uniform(streams_of[6], (CHANNELS, POINTS), jnp.float32) ** block_levels(streams_of[6], (CHANNELS, POINTS), ((1, 16),), -0.2, 0.2)), 2.0, 64.0),
    }


def reference(control_vec, ens_perturb, loc_blocks, tile_index, obs_weight, channel_level_mask, obs_precision):
    row_total = MEMBERS * LEVELS
    tile_count = POINTS // TILE
    tile_ids = jnp.arange(tile_count).astype(jnp.int32)
    control_low = control_vec.astype(jnp.bfloat16).reshape(row_total, tile_count, TILE)

    def forward_tile(tile_no):
        picked = jnp.take(control_low, tile_index[tile_no], axis=1).reshape(row_total, NEIGH * TILE)
        return jnp.dot(picked, loc_blocks[tile_no].reshape(NEIGH * TILE, TILE), preferred_element_type=jnp.float32)
    localized = lax.map(forward_tile, tile_ids)
    localized = jnp.moveaxis(localized, 0, 1).reshape(MEMBERS, LEVELS, POINTS).astype(jnp.bfloat16)
    ens_scale = 1.0 / math.sqrt(MEMBERS - 1)
    ensemble_level_block = jnp.moveaxis(ens_perturb, 2, 0)
    loc_levels = jnp.moveaxis(localized, 1, 0)

    def incr_level(pair):
        ensemble, weights = pair
        return jnp.einsum('mvp,mp->vp', ensemble.astype(jnp.float32), weights.astype(jnp.float32))
    analysis_increment = (lax.map(incr_level, (ensemble_level_block, loc_levels)) * ens_scale).astype(jnp.bfloat16)
    operator = obs_weight * channel_level_mask.astype(jnp.bfloat16)
    op_flat = operator.reshape(VARS * LEVELS, CHANNELS)
    inc_flat = jnp.moveaxis(analysis_increment, 1, 0).reshape(VARS * LEVELS, POINTS)
    evolved = jnp.dot(op_flat.T, inc_flat, preferred_element_type=jnp.float32)
    weighted = (obs_precision * evolved).astype(jnp.bfloat16)
    gradient = jnp.dot(op_flat, weighted, preferred_element_type=jnp.float32).astype(jnp.bfloat16)
    grad_levels = jnp.moveaxis(gradient.reshape(VARS, LEVELS, POINTS), 1, 0)

    def backward_level_rows(pair):
        ensemble, grad_lev = pair
        return jnp.einsum('mvp,vp->mp', ensemble.astype(jnp.float32), grad_lev.astype(jnp.float32))
    backward_values = (lax.map(backward_level_rows, (ensemble_level_block, grad_levels)) * ens_scale).astype(jnp.bfloat16)
    backward_values = jnp.moveaxis(backward_values, 0, 1).reshape(row_total, tile_count, TILE)

    def adjoint_tile(running, tile_no):
        block_t = loc_blocks[tile_no].transpose(2, 0, 1).reshape(TILE, NEIGH * TILE)
        part_vals = jnp.dot(backward_values[:, tile_no], block_t, preferred_element_type=jnp.float32)
        part_vals = part_vals.reshape(row_total, NEIGH, TILE)
        return (running.at[:, tile_index[tile_no]].add(part_vals), None)
    adjoint, _ = lax.scan(adjoint_tile, jnp.zeros((row_total, tile_count, TILE), jnp.float32), tile_ids)
    return control_vec + adjoint.reshape(MEMBERS, LEVELS, POINTS)
```

```python
import functools
import math

import jax
import jax.numpy as jnp
from jax import lax
from jax.experimental import pallas as pl
from jax.experimental.pallas import tpu as pltpu
from jax.sharding import PartitionSpec as P

MESH = pl.DeviceIdType.MESH
TILE = 128
PAD = 32


def exchange_kernel(
    geo, idx_ref, ctrl_hbm, ens_hbm, loc_hbm, obs_ref, mask_ref, prec_ref, back_hbm,
    ctrl32, ctrl, loc, ens, send, recv, bsend, opg, incg,
    ctrl_sem, loc_sem, ens_sem, own_sem, fsend, frecv, bsend_sem, brecv_sem, osend, orecv, isend, irecv,
):
    n_mem, n_lev, chunks, neigh, scale = geo
    me = lax.axis_index("mem")
    lev = lax.axis_index("lev")
    rows = ctrl32.shape[0]
    tiles = ctrl.shape[0]
    members = n_mem * (rows // 8)
    per_dev = rows * 3
    groups = ctrl_sem.shape[0]
    span = ctrl32.shape[1] // groups

    def peer(i, sign):
        dx, dz, dc = 3 - i % 4, 1 - i // 8, 1 - (i // 4) % 2
        x, z, c = me // 4, (me // 2) % 2, me % 2
        return ((x + sign * dx + 4) % 4) * 4 + ((z + dz) % 2) * 2 + (c + dc) % 2

    barrier = pltpu.get_barrier_semaphore()
    for i in range(n_mem - 1):
        pl.semaphore_signal(barrier, inc=1, device_id={"mem": peer(i, 1)}, device_id_type=MESH)
    for j in range(1, n_lev):
        pl.semaphore_signal(barrier, inc=1, device_id={"lev": (lev + j) % n_lev}, device_id_type=MESH)

    def ctrl_copy(g):
        cols = pl.ds(pl.multiple_of(g * span, TILE), span)
        return pltpu.make_async_copy(ctrl_hbm.at[:, cols], ctrl32.at[:, cols], ctrl_sem.at[g])

    def loc_copy(n):
        t = peer(n % n_mem, 1) * chunks + n // n_mem
        return pltpu.make_async_copy(loc_hbm.at[t], loc.at[t], loc_sem.at[n])

    def start(fn):
        def go(n, carry):
            fn(n).start()
            return carry
        return go

    lax.fori_loop(0, groups, start(ctrl_copy), 0)
    lax.fori_loop(0, tiles, start(loc_copy), 0)
    ens_copy = pltpu.make_async_copy(ens_hbm, ens, ens_sem)
    ens_copy.start()

    op = obs_ref[...].astype(jnp.float32) * mask_ref[...].astype(jnp.float32)[None]
    op = op.reshape(24, op.shape[2])
    op = jnp.concatenate([op, jnp.zeros((PAD - 24, op.shape[1]), jnp.float32)], axis=0)
    mine = pl.ds(pl.multiple_of(lev * PAD, PAD), PAD)
    opg[mine, :] = op.astype(jnp.bfloat16)

    per_group = span // TILE

    def convert(g, carry):
        ctrl_copy(g).wait()
        for u in range(per_group):
            s = g * per_group + u
            cols = pl.ds(pl.multiple_of(s * TILE, TILE), TILE)
            ctrl[s] = ctrl32[:, cols].astype(jnp.bfloat16)
        return carry

    lax.fori_loop(0, groups, convert, 0)
    pl.semaphore_wait(barrier, n_mem - 1 + n_lev - 1)

    def op_copy(j):
        return pltpu.make_async_remote_copy(
            src_ref=opg.at[mine], dst_ref=opg.at[mine], send_sem=osend.at[j], recv_sem=orecv.at[j],
            device_id={"lev": (lev + j) % n_lev}, device_id_type=MESH,
        )

    def inc_copy(c, j):
        return pltpu.make_async_remote_copy(
            src_ref=incg.at[c, mine], dst_ref=incg.at[c, mine],
            send_sem=isend.at[c, j], recv_sem=irecv.at[c, j],
            device_id={"lev": (lev + j) % n_lev}, device_id_type=MESH,
        )

    def fwd_copy(c, i):
        d = peer(i, 1)
        return pltpu.make_async_remote_copy(
            src_ref=send.at[c, d], dst_ref=recv.at[c, me], send_sem=fsend.at[c, i], recv_sem=frecv.at[c, i],
            device_id={"mem": d}, device_id_type=MESH,
        )

    def bwd_copy(c, i):
        d = peer(i, 1)
        return pltpu.make_async_remote_copy(
            src_ref=bsend.at[c, d], dst_ref=back_hbm.at[c, me], send_sem=bsend_sem.at[c, i],
            recv_sem=brecv_sem.at[c, i], device_id={"mem": d}, device_id_type=MESH,
        )

    for j in range(1, n_lev):
        op_copy(j).start()

    def localize(c, i):
        t = peer(i, 1) * chunks + c
        loc_copy(c * n_mem + i).wait()
        picked = jnp.concatenate([ctrl[idx_ref[t, k]] for k in range(neigh)], axis=1)
        out = jnp.dot(picked, loc[t], preferred_element_type=jnp.float32)
        return out.astype(jnp.bfloat16)

    def fwd(c):
        def step(i, carry):
            send[c, peer(i, 1)] = localize(c, i)
            fwd_copy(c, i).start()
            return carry

        lax.fori_loop(0, n_mem - 1, step, 0)
        recv[c, me] = localize(c, n_mem - 1)

    def part(c, src, acc):
        cols = pl.ds(c * TILE, TILE)
        weights = recv[c, src].astype(jnp.float32).reshape(rows // 8, 1, 8, TILE)
        pert = ens[pl.ds(pl.multiple_of(src * per_dev, per_dev), per_dev), cols]
        pert = pert.astype(jnp.float32).reshape(rows // 8, 3, 8, TILE)
        return acc + jnp.sum(pert * weights, axis=0)

    def increment(c):
        acc = part(c, me, jnp.zeros((3, 8, TILE), jnp.float32))

        def step(i, acc):
            fwd_copy(c, i).wait_recv()
            return part(c, peer(i, -1), acc)

        acc = lax.fori_loop(0, n_mem - 1, step, acc) * scale
        acc = jnp.concatenate([acc.reshape(24, TILE), jnp.zeros((PAD - 24, TILE), jnp.float32)], axis=0)
        incg[c, mine, :] = acc.astype(jnp.bfloat16)
        for j in range(1, n_lev):
            inc_copy(c, j).start()

    def observe(c):
        for j in range(1, n_lev):
            inc_copy(c, j).wait_recv()
        evolved = lax.dot_general(
            opg[...], incg[c], (((0,), (0,)), ((), ())), preferred_element_type=jnp.float32
        )
        weighted = (prec_ref[:, pl.ds(c * TILE, TILE)] * evolved).astype(jnp.bfloat16)
        grad = jnp.dot(opg[mine, :], weighted, preferred_element_type=jnp.float32)
        grad = grad.astype(jnp.bfloat16).astype(jnp.float32)[:24].reshape(1, 3, 8, TILE)

        def back(d):
            cols = pl.ds(c * TILE, TILE)
            pert = ens[pl.ds(pl.multiple_of(d * per_dev, per_dev), per_dev), cols]
            pert = pert.astype(jnp.float32).reshape(rows // 8, 3, 8, TILE)
            out = jnp.sum(pert * grad, axis=1) * scale
            bsend[c, d] = out.reshape(rows, TILE).astype(jnp.bfloat16)

        def step(i, carry):
            back(peer(i, 1))
            bwd_copy(c, i).start()
            return carry

        lax.fori_loop(0, n_mem - 1, step, 0)
        back(me)
        pltpu.make_async_copy(bsend.at[c, me], back_hbm.at[c, me], own_sem.at[c]).start()

    for c in range(chunks):
        fwd(c)
    ens_copy.wait()
    for j in range(1, n_lev):
        op_copy(j).wait()
    for c in range(chunks):
        increment(c)
        observe(c)

    for c in range(chunks):
        pltpu.make_async_copy(bsend.at[c, me], back_hbm.at[c, me], own_sem.at[c]).wait()

        def finish(i, carry):
            fwd_copy(c, i).wait_send()
            bwd_copy(c, i).wait()
            return carry

        lax.fori_loop(0, n_mem - 1, finish, 0)
        for j in range(1, n_lev):
            inc_copy(c, j).wait_send()


def adjoint_kernel(chunks, neigh, idx_ref, ctrl_hbm, back_ref, loc_hbm, out_hbm, acc, loc, ctrl_sem, loc_sem, out_sem):
    tiles = loc.shape[0]
    groups = loc_sem.shape[0]
    per_group = tiles // groups

    def loc_copy(g):
        at = pl.ds(g * per_group, per_group)
        return pltpu.make_async_copy(loc_hbm.at[at], loc.at[at], loc_sem.at[g])

    ctrl_copy = pltpu.make_async_copy(ctrl_hbm, acc, ctrl_sem)
    loc_copy(0).start()
    ctrl_copy.start()
    for g in range(1, groups):
        loc_copy(g).start()
    ctrl_copy.wait()

    def group(g, carry):
        loc_copy(g).wait()
        for u in range(per_group):
            t = g * per_group + u
            vals = lax.dot_general(
                back_ref[t % chunks, t // chunks], loc[t], (((1,), (1,)), ((), ())),
                preferred_element_type=jnp.float32,
            )
            for k in range(neigh):
                cols = pl.ds(pl.multiple_of(idx_ref[t, k] * TILE, TILE), TILE)
                acc[:, cols] += vals[:, k * TILE : (k + 1) * TILE]
        return carry

    lax.fori_loop(0, groups, group, 0)
    out = pltpu.make_async_copy(acc, out_hbm, out_sem)
    out.start()
    out.wait()


def body(n_mem, n_lev, control_vec, ens_perturb, loc_blocks, tile_index, obs_weight, channel_level_mask, obs_precision):
    mem_rows, lev_rows, points = control_vec.shape
    members = ens_perturb.shape[0]
    tiles, neigh = tile_index.shape
    chunks = tiles // n_mem
    rows = mem_rows * lev_rows
    channels = obs_weight.shape[2]
    control = control_vec.reshape(rows, points)
    ens = ens_perturb.reshape(members * 3 * lev_rows, points // n_mem)
    loc = loc_blocks.reshape(tiles, neigh * TILE, TILE)
    hbm = pl.BlockSpec(memory_space=pl.ANY)
    vmem = pl.BlockSpec(memory_space=pltpu.VMEM)
    smem = pl.BlockSpec(memory_space=pltpu.SMEM)
    dma = pltpu.SemaphoreType.DMA
    geo = (n_mem, n_lev, chunks, neigh, 1.0 / math.sqrt(members - 1))
    wide = (chunks, n_mem, rows, TILE)
    back = pl.pallas_call(
        functools.partial(exchange_kernel, geo),
        out_shape=jax.ShapeDtypeStruct(wide, jnp.bfloat16),
        in_specs=[smem, hbm, hbm, hbm, vmem, vmem, vmem],
        out_specs=hbm,
        scratch_shapes=[
            pltpu.VMEM((rows, points), jnp.float32),
            pltpu.VMEM((tiles, rows, TILE), jnp.bfloat16),
            pltpu.VMEM(loc.shape, jnp.bfloat16),
            pltpu.VMEM(ens.shape, jnp.bfloat16),
            pltpu.VMEM(wide, jnp.bfloat16),
            pltpu.VMEM(wide, jnp.bfloat16),
            pltpu.VMEM(wide, jnp.bfloat16),
            pltpu.VMEM((n_lev * PAD, channels), jnp.bfloat16),
            pltpu.VMEM((chunks, n_lev * PAD, TILE), jnp.bfloat16),
            dma((8,)), dma((tiles,)), dma, dma((chunks,)),
            dma((chunks, n_mem)), dma((chunks, n_mem)), dma((chunks, n_mem)), dma((chunks, n_mem)),
            dma((n_lev,)), dma((n_lev,)), dma((chunks, n_lev)), dma((chunks, n_lev)),
        ],
        compiler_params=pltpu.CompilerParams(
            collective_id=0, has_side_effects=True, vmem_limit_bytes=56 * 2**20
        ),
        name="exchange",
    )(tile_index, control, ens, loc, obs_weight, channel_level_mask, obs_precision)
    out = pl.pallas_call(
        functools.partial(adjoint_kernel, chunks, neigh),
        out_shape=jax.ShapeDtypeStruct((rows, points), jnp.float32),
        in_specs=[smem, hbm, vmem, hbm],
        out_specs=hbm,
        scratch_shapes=[
            pltpu.VMEM((rows, points), jnp.float32),
            pltpu.VMEM(loc.shape, jnp.bfloat16),
            dma, dma((16,)), dma,
        ],
        compiler_params=pltpu.CompilerParams(vmem_limit_bytes=48 * 2**20),
        name="adjoint",
    )(tile_index, control, back, loc)
    return out.reshape(control_vec.shape)


def solution(mesh):
    return jax.shard_map(
        functools.partial(body, mesh.shape["mem"], mesh.shape["lev"]),
        mesh=mesh,
        in_specs=(
            P("mem", "lev", None),
            P(None, None, "lev", "mem"),
            P(),
            P(),
            P(None, "lev", None),
            P("lev", None),
            P(None, "mem"),
        ),
        out_specs=P("mem", "lev", None),
        check_vma=False,
    )
```

```python
import functools
import math

import jax
import jax.numpy as jnp
from jax import lax
from jax.experimental import pallas as pl
from jax.experimental.pallas import tpu as pltpu
from jax.sharding import PartitionSpec as P

MESH = pl.DeviceIdType.MESH
TILE = 128
PAD = 32
AHEAD = 3


def exchange_kernel(
    geo, idx_ref, ctrl_hbm, ens_hbm, loc_hbm, obs_ref, mask_ref, prec_hbm, back_hbm,
    prec_ref, prec_sem, ctrl32, ctrl, loc, ens, send, recv, bsend, opg, incg,
    ctrl_sem, loc_sem, ens_sem, own_sem, fsend, frecv, bsend_sem, brecv_sem, osend, orecv, isend, irecv,
):
    n_mem, n_lev, chunks, neigh, scale = geo
    me = lax.axis_index("mem")
    lev = lax.axis_index("lev")
    my_x, my_z, my_c = lax.div(me, 4), lax.rem(lax.div(me, 2), 2), lax.rem(me, 2)
    rows = ctrl32.shape[0]
    per_dev = rows * 3
    groups = ctrl_sem.shape[0]
    span = ctrl32.shape[1] // groups

    def zc_of(g):
        return lax.rem(my_z + 1 - lax.div(g, 2), 2) * 2 + lax.rem(my_c + 1 - lax.rem(g, 2), 2)

    def peer(i):
        return lax.rem(my_x + 3 - lax.rem(i, 4), 4) * 4 + zc_of(lax.div(i, 4))

    def source(i):
        return lax.rem(my_x + 1 + lax.rem(i, 4), 4) * 4 + zc_of(lax.div(i, 4))

    def level_peer(j):
        return {"lev": lax.rem(lev + j, n_lev)}

    def ctrl_copy(g):
        cols = pl.ds(pl.multiple_of(g * span, TILE), span)
        return pltpu.make_async_copy(ctrl_hbm.at[:, cols], ctrl32.at[:, cols], ctrl_sem.at[g])

    def loc_copy(n):
        c, zc = lax.div(n, 4), zc_of(lax.rem(n, 4))
        return pltpu.make_async_copy(loc_hbm.at[:, zc, c], loc.at[c, zc], loc_sem.at[n])

    def repeat(lo, hi, fn):
        def step(n, carry):
            fn(n)
            return carry

        lax.fori_loop(lo, hi, step, 0)

    repeat(0, groups, lambda g: ctrl_copy(g).start())
    loc_copy(0).start()
    barrier = pltpu.get_barrier_semaphore()
    for i in range(n_mem - 1):
        pl.semaphore_signal(barrier, inc=1, device_id={"mem": peer(i)}, device_id_type=MESH)
    for j in range(1, n_lev):
        pl.semaphore_signal(barrier, inc=1, device_id=level_peer(j), device_id_type=MESH)
    ens_copy = pltpu.make_async_copy(ens_hbm, ens, ens_sem)
    prec_copy = pltpu.make_async_copy(prec_hbm, prec_ref, prec_sem)

    op = obs_ref[...].astype(jnp.float32) * mask_ref[...].astype(jnp.float32)[None]
    op = op.reshape(24, op.shape[2])
    op = jnp.concatenate([op, jnp.zeros((PAD - 24, op.shape[1]), jnp.float32)], axis=0)
    mine = pl.ds(pl.multiple_of(lev * PAD, PAD), PAD)
    opg[mine, :] = op.astype(jnp.bfloat16)

    per_group = span // TILE

    def convert(g):
        ctrl_copy(g).wait()
        loc_copy(g + 1).start()
        for u in range(per_group):
            s = g * per_group + u
            cols = pl.ds(pl.multiple_of(s * TILE, TILE), TILE)
            ctrl[s] = ctrl32[:, cols].astype(jnp.bfloat16)

    repeat(0, groups, convert)

    def op_copy(j):
        return pltpu.make_async_remote_copy(
            src_ref=opg.at[mine], dst_ref=opg.at[mine], send_sem=osend.at[j], recv_sem=orecv.at[j],
            device_id=level_peer(j), device_id_type=MESH,
        )

    def inc_copy(c, j):
        return pltpu.make_async_remote_copy(
            src_ref=incg.at[c, mine], dst_ref=incg.at[c, mine],
            send_sem=isend.at[c, j], recv_sem=irecv.at[c, j],
            device_id=level_peer(j), device_id_type=MESH,
        )

    def fwd_copy(c, i):
        d = peer(i)
        return pltpu.make_async_remote_copy(
            src_ref=send.at[c, d], dst_ref=recv.at[c, me], send_sem=fsend.at[c, i], recv_sem=frecv.at[c, i],
            device_id={"mem": d}, device_id_type=MESH,
        )

    def bwd_copy(c, i):
        d = peer(i)
        return pltpu.make_async_remote_copy(
            src_ref=bsend.at[c, d], dst_ref=back_hbm.at[c, me], send_sem=bsend_sem.at[c, i],
            recv_sem=brecv_sem.at[c, i], device_id={"mem": d}, device_id_type=MESH,
        )

    def localize(n):
        c, zc = lax.div(n, 4), zc_of(lax.rem(n, 4))
        loc_copy(n).wait()
        for u in range(4):
            x = lax.rem(my_x + 3 - u, 4)
            d = x * 4 + zc
            t = d * chunks + c
            picked = jnp.concatenate([ctrl[idx_ref[k, t]] for k in range(neigh)], axis=1)
            out = jnp.dot(picked, loc[c, zc, x], preferred_element_type=jnp.float32)
            send[c, d] = out.astype(jnp.bfloat16)

    def part(c, values, src, acc):
        cols = pl.ds(c * TILE, TILE)
        weights = values[c, src].astype(jnp.float32).reshape(rows // 8, 1, 8, TILE)
        pert = ens[pl.ds(pl.multiple_of(src * per_dev, per_dev), per_dev), cols]
        pert = pert.astype(jnp.float32).reshape(rows // 8, 3, 8, TILE)
        return acc + jnp.sum(pert * weights, axis=0)

    def increment(c):
        acc = part(c, send, me, jnp.zeros((3, 8, TILE), jnp.float32))

        def step(i, acc):
            fwd_copy(c, i).wait_recv()
            return part(c, recv, source(i), acc)

        acc = lax.fori_loop(0, n_mem - 1, step, acc) * scale
        acc = jnp.concatenate([acc.reshape(24, TILE), jnp.zeros((PAD - 24, TILE), jnp.float32)], axis=0)
        incg[c, mine, :] = acc.astype(jnp.bfloat16)
        repeat(1, n_lev, lambda j: inc_copy(c, j).start())

    def observe(c):
        repeat(1, n_lev, lambda j: inc_copy(c, j).wait_recv())
        cols = pl.ds(c * TILE, TILE)
        evolved = lax.dot_general(
            opg[...], incg[c], (((0,), (0,)), ((), ())), preferred_element_type=jnp.float32
        )
        weighted = (prec_ref[:, cols] * evolved).astype(jnp.bfloat16)
        grad = jnp.dot(opg[mine, :], weighted, preferred_element_type=jnp.float32)
        grad = grad.astype(jnp.bfloat16).astype(jnp.float32)[:24].reshape(1, 3, 8, TILE)

        def back(d):
            pert = ens[pl.ds(pl.multiple_of(d * per_dev, per_dev), per_dev), cols]
            pert = pert.astype(jnp.float32).reshape(rows // 8, 3, 8, TILE)
            out = jnp.sum(pert * grad, axis=1) * scale
            bsend[c, d] = out.reshape(rows, TILE).astype(jnp.bfloat16)

        repeat(0, n_mem, back)

    half = n_mem // 2

    def send_fwd(c, lo=0, hi=n_mem - 1):
        repeat(lo, hi, lambda i: fwd_copy(c, i).start())

    def own_copy(c):
        return pltpu.make_async_copy(bsend.at[c, me], back_hbm.at[c, me], own_sem.at[c])

    def send_bwd(c, lo=0, hi=n_mem - 1):
        repeat(lo, hi, lambda i: bwd_copy(c, i).start())
        if lo == 0:
            own_copy(c).start()

    def first(n):
        loc_copy(n + groups + 1).start()
        localize(n)

    def send_group(n):
        c, g = lax.div(n, 4), lax.rem(n, 4)
        for u in range(4):
            if u < 3:
                fwd_copy(c, g * 4 + u).start()
            else:
                pl.when(g < 3)(lambda: fwd_copy(c, g * 4 + 3).start())

    def first_sent(n):
        first(n)
        send_group(n)

    def later_sent(n):
        localize(n)
        send_group(n)

    repeat(0, 4, first)
    pl.semaphore_wait(barrier, n_mem - 1 + n_lev - 1)
    send_fwd(0)
    repeat(1, n_lev, lambda j: op_copy(j).start())
    repeat(4, chunks * 4 - groups - 1, first_sent)
    ens_copy.start()
    prec_copy.start()
    later_sent(chunks * 4 - groups - 1)
    repeat(8, 10, later_sent)
    repeat(10, 16, localize)
    ens_copy.wait()
    prec_copy.wait()
    increment(0)
    send_fwd(2, half)
    send_fwd(3, 0, half)
    increment(1)
    send_fwd(3, half)
    repeat(1, n_lev, lambda j: op_copy(j).wait())
    observe(0)
    send_bwd(0, 0, half)
    increment(2)
    send_bwd(0, half)
    observe(1)
    send_bwd(1, 0, half)
    increment(3)
    send_bwd(1, half)
    observe(2)
    send_bwd(2)
    observe(3)
    send_bwd(3)

    for c in range(chunks):
        own_copy(c).wait()

        def finish(i):
            fwd_copy(c, i).wait_send()
            bwd_copy(c, i).wait()

        repeat(0, n_mem - 1, finish)
        repeat(1, n_lev, lambda j: inc_copy(c, j).wait_send())


def adjoint_kernel(chunks, neigh, idx_ref, ctrl_hbm, back_ref, loc_hbm, out_hbm, acc, loc, ctrl_sem, loc_sem, out_sem):
    tiles = loc.shape[0]
    groups = loc_sem.shape[0]
    per_group = tiles // groups

    def loc_copy(g):
        at = pl.ds(g * per_group, per_group)
        return pltpu.make_async_copy(loc_hbm.at[at], loc.at[at], loc_sem.at[g])

    ctrl_copy = pltpu.make_async_copy(ctrl_hbm, acc, ctrl_sem)
    ctrl_copy.start()
    for g in range(AHEAD):
        loc_copy(g).start()
    ctrl_copy.wait()

    def group(g, carry):
        @pl.when(g + AHEAD < groups)
        def _():
            loc_copy(g + AHEAD).start()

        loc_copy(g).wait()
        for u in range(per_group):
            t = g * per_group + u
            vals = lax.dot_general(
                back_ref[t % chunks, t // chunks], loc[t], (((1,), (1,)), ((), ())),
                preferred_element_type=jnp.float32,
            )
            for k in range(neigh):
                cols = pl.ds(pl.multiple_of(idx_ref[k, t] * TILE, TILE), TILE)
                acc[:, cols] += vals[:, k * TILE : (k + 1) * TILE]
        return carry

    lax.fori_loop(0, groups, group, 0)
    out = pltpu.make_async_copy(acc, out_hbm, out_sem)
    out.start()
    out.wait()


def body(n_mem, n_lev, control_vec, ens_perturb, loc_blocks, tile_index, obs_weight, channel_level_mask, obs_precision):
    mem_rows, lev_rows, points = control_vec.shape
    members = ens_perturb.shape[0]
    tiles, neigh = tile_index.shape
    chunks = tiles // n_mem
    rows = mem_rows * lev_rows
    channels = obs_weight.shape[2]
    control = control_vec.reshape(rows, points)
    index = tile_index.T
    ens = ens_perturb.reshape(members * 3 * lev_rows, points // n_mem)
    loc = loc_blocks.reshape(tiles, neigh * TILE, TILE)
    hbm = pl.BlockSpec(memory_space=pl.ANY)
    vmem = pl.BlockSpec(memory_space=pltpu.VMEM)
    smem = pl.BlockSpec(memory_space=pltpu.SMEM)
    dma = pltpu.SemaphoreType.DMA
    geo = (n_mem, n_lev, chunks, neigh, 1.0 / math.sqrt(members - 1))
    wide = (chunks, n_mem, rows, TILE)
    back = pl.pallas_call(
        functools.partial(exchange_kernel, geo),
        out_shape=jax.ShapeDtypeStruct(wide, jnp.bfloat16),
        in_specs=[smem, hbm, hbm, hbm, vmem, vmem, hbm],
        out_specs=hbm,
        scratch_shapes=[
            pltpu.VMEM(obs_precision.shape, jnp.float32),
            dma,
            pltpu.VMEM((rows, points), jnp.float32),
            pltpu.VMEM((tiles, rows, TILE), jnp.bfloat16),
            pltpu.VMEM((chunks, 4, 4, neigh * TILE, TILE), jnp.bfloat16),
            pltpu.VMEM(ens.shape, jnp.bfloat16),
            pltpu.VMEM(wide, jnp.bfloat16),
            pltpu.VMEM(wide, jnp.bfloat16),
            pltpu.VMEM(wide, jnp.bfloat16),
            pltpu.VMEM((n_lev * PAD, channels), jnp.bfloat16),
            pltpu.VMEM((chunks, n_lev * PAD, TILE), jnp.bfloat16),
            dma((8,)), dma((chunks * 4,)), dma, dma((chunks,)),
            dma((chunks, n_mem)), dma((chunks, n_mem)), dma((chunks, n_mem)), dma((chunks, n_mem)),
            dma((n_lev,)), dma((n_lev,)), dma((chunks, n_lev)), dma((chunks, n_lev)),
        ],
        compiler_params=pltpu.CompilerParams(
            collective_id=0, has_side_effects=True, vmem_limit_bytes=56 * 2**20
        ),
        name="exchange",
    )(index, control, ens, loc.reshape(4, 4, chunks, neigh * TILE, TILE), obs_weight, channel_level_mask, obs_precision)
    out = pl.pallas_call(
        functools.partial(adjoint_kernel, chunks, neigh),
        out_shape=jax.ShapeDtypeStruct((rows, points), jnp.float32),
        in_specs=[smem, hbm, vmem, hbm],
        out_specs=hbm,
        scratch_shapes=[
            pltpu.VMEM((rows, points), jnp.float32),
            pltpu.VMEM(loc.shape, jnp.bfloat16),
            dma, dma((16,)), dma,
        ],
        compiler_params=pltpu.CompilerParams(vmem_limit_bytes=48 * 2**20),
        name="adjoint",
    )(index, control, back, loc)
    return out.reshape(control_vec.shape)


def solution(mesh):
    return jax.shard_map(
        functools.partial(body, mesh.shape["mem"], mesh.shape["lev"]),
        mesh=mesh,
        in_specs=(
            P("mem", "lev", None),
            P(None, None, "lev", "mem"),
            P(),
            P(),
            P(None, "lev", None),
            P("lev", None),
            P(None, "mem"),
        ),
        out_specs=P("mem", "lev", None),
        check_vma=False,
    )
```

```python
import functools
import math

import jax
import jax.numpy as jnp
from jax import lax
from jax.experimental import pallas as pl
from jax.experimental.pallas import tpu as pltpu
from jax.sharding import PartitionSpec as P

MESH = pl.DeviceIdType.MESH
TILE = 128
PAD = 32
KEEP = 3
SLOTS = 104
WAYS = 16
UNROLL = 13


def exchange_kernel(
    geo, idx_ref, idx_vec, ctrl_hbm, ens_hbm, loc_hbm, obs_ref, mask_ref, prec_hbm, back_hbm, part_hbm,
    arrived0, arrived1, arrived2, sums, table_vec, table, table_sem, part_sem, prec_ref, prec_sem, ctrl32, ctrl, loc, ens, send, recv, bsend, opg, incg,
    ctrl_sem, loc_sem, ens_sem, own_sem, fsend, frecv, bsend_sem, brecv_sem, osend, orecv, isend, irecv,
):
    n_mem, n_lev, chunks, neigh, scale = geo
    arrived = (arrived0, arrived1, arrived2)
    me = lax.axis_index("mem")
    lev = lax.axis_index("lev")
    my_x, my_z, my_c = lax.div(me, 4), lax.rem(lax.div(me, 2), 2), lax.rem(me, 2)
    rows = ctrl32.shape[0]
    per_dev = rows * 3
    groups = ctrl_sem.shape[0]
    span = ctrl32.shape[1] // groups

    def zc_of(g):
        return lax.rem(my_z + 1 - lax.div(g, 2), 2) * 2 + lax.rem(my_c + 1 - lax.rem(g, 2), 2)

    def peer(i):
        return lax.rem(my_x + 3 - lax.rem(i, 4), 4) * 4 + zc_of(lax.div(i, 4))

    def source(i):
        return lax.rem(my_x + 1 + lax.rem(i, 4), 4) * 4 + zc_of(lax.div(i, 4))

    def level_peer(j):
        return {"lev": lax.rem(lev + j, n_lev)}

    def ctrl_copy(g):
        cols = pl.ds(pl.multiple_of(g * span, TILE), span)
        return pltpu.make_async_copy(ctrl_hbm.at[:, cols], ctrl32.at[:, cols], ctrl_sem.at[g])

    def loc_copy(n):
        c, zc = lax.div(n, 4), zc_of(lax.rem(n, 4))
        return pltpu.make_async_copy(loc_hbm.at[:, zc, c], loc.at[c, zc], loc_sem.at[n])

    def repeat(lo, hi, fn):
        def step(n, carry):
            fn(n)
            return carry

        lax.fori_loop(lo, hi, step, 0)

    repeat(0, groups, lambda g: ctrl_copy(g).start())
    loc_copy(0).start()
    barrier = pltpu.get_barrier_semaphore()
    for i in range(n_mem - 1):
        pl.semaphore_signal(barrier, inc=1, device_id={"mem": peer(i)}, device_id_type=MESH)
    for j in range(1, n_lev):
        pl.semaphore_signal(barrier, inc=1, device_id=level_peer(j), device_id_type=MESH)
    ens_copy = pltpu.make_async_copy(ens_hbm, ens, ens_sem)
    prec_copy = pltpu.make_async_copy(prec_hbm, prec_ref, prec_sem)

    op = obs_ref[...].astype(jnp.float32) * mask_ref[...].astype(jnp.float32)[None]
    op = op.reshape(24, op.shape[2])
    op = jnp.concatenate([op, jnp.zeros((PAD - 24, op.shape[1]), jnp.float32)], axis=0)
    mine = pl.ds(pl.multiple_of(lev * PAD, PAD), PAD)
    opg[mine, :] = op.astype(jnp.bfloat16)

    per_group = span // TILE

    def convert(g):
        ctrl_copy(g).wait()
        loc_copy(g + 1).start()
        for u in range(per_group):
            s = g * per_group + u
            cols = pl.ds(pl.multiple_of(s * TILE, TILE), TILE)
            ctrl[s] = ctrl32[:, cols].astype(jnp.bfloat16)

    repeat(0, groups, convert)

    def tabulate(c):
        target = lax.broadcasted_iota(jnp.int32, (64, 64), 0)
        idx = idx_vec[...]
        hits = jnp.zeros((64, 64), jnp.int32)
        for k in range(neigh):
            hits = hits + jnp.where(target == idx[k : k + 1, :], k + 1, 0)
        hits = jnp.minimum(hits, neigh)
        lane = lax.broadcasted_iota(jnp.int32, (64, TILE), 1)

        def column(d):
            at = d * chunks + c
            return jnp.broadcast_to(hits[:, at : at + 1], (64, TILE))

        count = jnp.zeros((64, TILE), jnp.int32)
        for d in range(n_mem):
            count = count + jnp.minimum(column(d), 1)
        pairs = lax.div(count + 1, 2)
        slot = lane[:1]
        end = jnp.zeros((1, TILE), jnp.int32)
        base = jnp.zeros((1, TILE), jnp.int32)
        for s in range(64):
            table_vec[c, 8 + s : 9 + s] = end
            end = end + pairs[s : s + 1]
            base = jnp.where(end <= slot, end, base)
        begin = table_vec[c, 8:]
        even = jnp.zeros((64, TILE), jnp.int32)
        odd = jnp.zeros((64, TILE), jnp.int32)
        seen = jnp.zeros((64, TILE), jnp.int32)
        for d in range(n_mem):
            value = column(d)
            here = jnp.where((lane == begin + lax.div(seen, 2)) & (value > 0), value + d * WAYS, 0)
            second = lax.rem(seen, 2)
            even = even + here * (1 - second)
            odd = odd + here * second
            seen = seen + jnp.minimum(value, 1)

        def codes(values):
            for size in (32, 16, 8):
                values = values[:size] + values[size:]
            total = values[0:1]
            for s in range(1, 8):
                total = total + values[s : s + 1]
            return jnp.where(total > 0, total - 1, WAYS * n_mem)

        row = lax.broadcasted_iota(jnp.int32, (8, TILE), 0)
        head = jnp.where(row == 0, codes(even), jnp.where(row == 1, codes(odd), slot - base))
        table_vec[c, :8] = head
        last = jnp.maximum(begin + pairs - 1, 0)
        table_vec[c, 8:] = jnp.where(lane == 1, jnp.minimum(count, 1), last)
        arrived[c][n_mem] = jnp.zeros((rows, TILE), jnp.bfloat16)

    table_copy = pltpu.make_async_copy(table_vec, table, table_sem)

    def op_copy(j):
        return pltpu.make_async_remote_copy(
            src_ref=opg.at[mine], dst_ref=opg.at[mine], send_sem=osend.at[j], recv_sem=orecv.at[j],
            device_id=level_peer(j), device_id_type=MESH,
        )

    def inc_copy(c, j):
        return pltpu.make_async_remote_copy(
            src_ref=incg.at[c, mine], dst_ref=incg.at[c, mine],
            send_sem=isend.at[c, j], recv_sem=irecv.at[c, j],
            device_id=level_peer(j), device_id_type=MESH,
        )

    def fwd_copy(c, i):
        d = peer(i)
        return pltpu.make_async_remote_copy(
            src_ref=send.at[c, d], dst_ref=recv.at[c, me], send_sem=fsend.at[c, i], recv_sem=frecv.at[c, i],
            device_id={"mem": d}, device_id_type=MESH,
        )

    def landing(c):
        return arrived[c].at[me] if c < KEEP else back_hbm.at[c - KEEP, me]

    def bwd_copy(c, i):
        d = peer(i)
        return pltpu.make_async_remote_copy(
            src_ref=bsend.at[c, d], dst_ref=landing(c), send_sem=bsend_sem.at[c, i],
            recv_sem=brecv_sem.at[c, i], device_id={"mem": d}, device_id_type=MESH,
        )

    def localize(n):
        c, zc = lax.div(n, 4), zc_of(lax.rem(n, 4))
        loc_copy(n).wait()
        for u in range(4):
            x = lax.rem(my_x + 3 - u, 4)
            d = x * 4 + zc
            t = d * chunks + c
            picked = jnp.concatenate([ctrl[idx_ref[k, t]] for k in range(neigh)], axis=1)
            out = jnp.dot(picked, loc[c, zc, x].reshape(neigh * TILE, TILE), preferred_element_type=jnp.float32)
            send[c, d] = out.astype(jnp.bfloat16)

    def part(c, values, src, acc):
        cols = pl.ds(c * TILE, TILE)
        weights = values[c, src].astype(jnp.float32).reshape(rows // 8, 1, 8, TILE)
        pert = ens[pl.ds(pl.multiple_of(src * per_dev, per_dev), per_dev), cols]
        pert = pert.astype(jnp.float32).reshape(rows // 8, 3, 8, TILE)
        return acc + jnp.sum(pert * weights, axis=0)

    def increment(c):
        acc = part(c, send, me, jnp.zeros((3, 8, TILE), jnp.float32))

        def step(i, acc):
            fwd_copy(c, i).wait_recv()
            return part(c, recv, source(i), acc)

        acc = lax.fori_loop(0, n_mem - 1, step, acc) * scale
        acc = jnp.concatenate([acc.reshape(24, TILE), jnp.zeros((PAD - 24, TILE), jnp.float32)], axis=0)
        incg[c, mine, :] = acc.astype(jnp.bfloat16)
        repeat(1, n_lev, lambda j: inc_copy(c, j).start())

    def observe(c):
        repeat(1, n_lev, lambda j: inc_copy(c, j).wait_recv())
        cols = pl.ds(c * TILE, TILE)
        evolved = lax.dot_general(
            opg[...], incg[c], (((0,), (0,)), ((), ())), preferred_element_type=jnp.float32
        )
        weighted = (prec_ref[:, cols] * evolved).astype(jnp.bfloat16)
        grad = jnp.dot(opg[mine, :], weighted, preferred_element_type=jnp.float32)
        grad = grad.astype(jnp.bfloat16).astype(jnp.float32)[:24].reshape(1, 3, 8, TILE)

        def back(d):
            pert = ens[pl.ds(pl.multiple_of(d * per_dev, per_dev), per_dev), cols]
            pert = pert.astype(jnp.float32).reshape(rows // 8, 3, 8, TILE)
            out = jnp.sum(pert * grad, axis=1) * scale
            bsend[c, d] = out.reshape(rows, TILE).astype(jnp.bfloat16)

        repeat(0, n_mem, back)

    half = n_mem // 2

    def send_fwd(c, lo=0, hi=n_mem - 1):
        repeat(lo, hi, lambda i: fwd_copy(c, i).start())

    def own_copy(c):
        return pltpu.make_async_copy(bsend.at[c, me], landing(c), own_sem.at[c])

    def send_bwd(c, lo=0, hi=n_mem - 1):
        repeat(lo, hi, lambda i: bwd_copy(c, i).start())
        if lo == 0:
            own_copy(c).start()

    def first(n):
        loc_copy(n + groups + 1).start()
        localize(n)

    def send_group(n):
        c, g = lax.div(n, 4), lax.rem(n, 4)
        for u in range(4):
            if u < 3:
                fwd_copy(c, g * 4 + u).start()
            else:
                pl.when(g < 3)(lambda: fwd_copy(c, g * 4 + 3).start())

    def first_sent(n):
        first(n)
        send_group(n)

    def later_sent(n):
        localize(n)
        send_group(n)

    def part_copy(g):
        cols = pl.ds(pl.multiple_of(g * span, TILE), span)
        return pltpu.make_async_copy(ctrl32.at[:, cols], part_hbm.at[:, cols], part_sem.at[g])

    def gather(c):
        own_copy(c).wait()
        repeat(0, n_mem - 1, lambda i: bwd_copy(c, i).wait_recv())

        def block(code):
            d, k = lax.div(code, WAYS), lax.rem(code, WAYS)
            x, zc = lax.rem(lax.div(d, 4), 4), lax.rem(d, 4)
            return arrived[c][d], loc[c, zc, x, k]

        def slots(q, before):
            for u in range(UNROLL):
                p = q * UNROLL + u
                left, right = zip(block(table[c, 0, p]), block(table[c, 1, p]))
                value = lax.dot_general(
                    jnp.concatenate(left, axis=1), jnp.concatenate(right, axis=1), (((1,), (1,)), ((), ())),
                    preferred_element_type=jnp.float32,
                )
                before = value + jnp.minimum(table[c, 2, p], 1).astype(jnp.float32) * before
                sums[p] = before
            return before

        lax.fori_loop(0, SLOTS // UNROLL, slots, jnp.zeros((rows, TILE), jnp.float32))

        def settle(g):
            for u in range(per_group):
                s = g * per_group + u
                cols = pl.ds(pl.multiple_of(s * TILE, TILE), TILE)
                present = table[c, 8 + s, 1].astype(jnp.float32)
                ctrl32[:, cols] += present * sums[table[c, 8 + s, 0]]
            if c == KEEP - 1:
                part_copy(g).start()

        repeat(0, groups, settle)

    repeat(0, 4, first)
    pl.semaphore_wait(barrier, n_mem - 1 + n_lev - 1)
    send_fwd(0)
    repeat(1, n_lev, lambda j: op_copy(j).start())
    repeat(4, chunks * 4 - groups - 1, first_sent)
    ens_copy.start()
    prec_copy.start()
    later_sent(chunks * 4 - groups - 1)
    repeat(8, 10, later_sent)
    repeat(10, 16, localize)
    ens_copy.wait()
    prec_copy.wait()
    increment(0)
    send_fwd(2, half)
    send_fwd(3, 0, half)
    increment(1)
    send_fwd(3, half)
    repeat(1, n_lev, lambda j: op_copy(j).wait())
    tabulate(0)
    tabulate(1)
    observe(0)
    send_bwd(0, 0, half)
    increment(2)
    send_bwd(0, half)
    observe(1)
    send_bwd(1, 0, half)
    tabulate(2)
    table_copy.start()
    increment(3)
    send_bwd(1, half)
    observe(2)
    send_bwd(2)
    table_copy.wait()
    gather(0)
    observe(3)
    send_bwd(3)
    for c in range(1, KEEP):
        gather(c)

    for c in range(chunks):
        if c >= KEEP:
            own_copy(c).wait()

        def finish(i):
            fwd_copy(c, i).wait_send()
            bwd_copy(c, i).wait_send()
            if c >= KEEP:
                bwd_copy(c, i).wait_recv()

        repeat(0, n_mem - 1, finish)
        repeat(1, n_lev, lambda j: inc_copy(c, j).wait_send())
    repeat(0, groups, lambda g: part_copy(g).wait())


def adjoint_kernel(
    chunks, neigh, idx_ref, part_hbm, back_hbm, loc_hbm, out_hbm, acc, back, loc, part_sem, back_sem, loc_sem, out_sem
):
    steps = loc_sem.shape[0]
    n_mem = back.shape[1]

    def loc_copy(n):
        return pltpu.make_async_copy(loc_hbm.at[n % n_mem, KEEP + n // n_mem], loc.at[n], loc_sem.at[n])

    back_copy = pltpu.make_async_copy(back_hbm, back, back_sem)
    part_copy = pltpu.make_async_copy(part_hbm, acc, part_sem)
    part_copy.start()
    back_copy.start()
    for n in range(steps):
        loc_copy(n).start()
    back_copy.wait()
    part_copy.wait()

    def group(g, carry):
        for u in range(4):
            loc_copy(g * 4 + u).wait()
        for u in range(4):
            n = g * 4 + u
            c, d = n // n_mem, n % n_mem
            t = d * chunks + c + KEEP
            vals = lax.dot_general(
                back[c, d], loc[n], (((1,), (1,)), ((), ())), preferred_element_type=jnp.float32
            )
            for k in range(neigh):
                cols = pl.ds(pl.multiple_of(idx_ref[k, t] * TILE, TILE), TILE)
                acc[:, cols] += vals[:, k * TILE : (k + 1) * TILE]
        return carry

    lax.fori_loop(0, steps // 4, group, 0)
    out = pltpu.make_async_copy(acc, out_hbm, out_sem)
    out.start()
    out.wait()


def body(n_mem, n_lev, control_vec, ens_perturb, loc_blocks, tile_index, obs_weight, channel_level_mask, obs_precision):
    mem_rows, lev_rows, points = control_vec.shape
    members = ens_perturb.shape[0]
    tiles, neigh = tile_index.shape
    chunks = tiles // n_mem
    rows = mem_rows * lev_rows
    channels = obs_weight.shape[2]
    control = control_vec.reshape(rows, points)
    index = tile_index.T
    ens = ens_perturb.reshape(members * 3 * lev_rows, points // n_mem)
    loc = loc_blocks.reshape(tiles, neigh * TILE, TILE)
    hbm = pl.BlockSpec(memory_space=pltpu.HBM)
    vmem = pl.BlockSpec(memory_space=pltpu.VMEM)
    smem = pl.BlockSpec(memory_space=pltpu.SMEM)
    dma = pltpu.SemaphoreType.DMA
    geo = (n_mem, n_lev, chunks, neigh, 1.0 / math.sqrt(members - 1))
    wide = (chunks, n_mem, rows, TILE)
    back, part = pl.pallas_call(
        functools.partial(exchange_kernel, geo),
        out_shape=(
            jax.ShapeDtypeStruct((chunks - KEEP,) + wide[1:], jnp.bfloat16),
            jax.ShapeDtypeStruct((rows, points), jnp.float32),
        ),
        in_specs=[smem, vmem, hbm, hbm, hbm, vmem, vmem, hbm],
        out_specs=(hbm, hbm),
        scratch_shapes=[
            *[pltpu.VMEM((n_mem + 1, rows, TILE), jnp.bfloat16)] * KEEP,
            pltpu.VMEM((SLOTS, rows, TILE), jnp.float32),
            pltpu.VMEM((KEEP, 72, TILE), jnp.int32),
            pltpu.SMEM((KEEP, 72, TILE), jnp.int32),
            dma,
            dma((8,)),
            pltpu.VMEM(obs_precision.shape, jnp.float32),
            dma,
            pltpu.VMEM((rows, points), jnp.float32),
            pltpu.VMEM((tiles, rows, TILE), jnp.bfloat16),
            pltpu.VMEM((chunks, 4, 4, neigh, TILE, TILE), jnp.bfloat16),
            pltpu.VMEM(ens.shape, jnp.bfloat16),
            pltpu.VMEM(wide, jnp.bfloat16),
            pltpu.VMEM(wide, jnp.bfloat16),
            pltpu.VMEM(wide, jnp.bfloat16),
            pltpu.VMEM((n_lev * PAD, channels), jnp.bfloat16),
            pltpu.VMEM((chunks, n_lev * PAD, TILE), jnp.bfloat16),
            dma((8,)), dma((chunks * 4,)), dma, dma((chunks,)),
            dma((chunks, n_mem)), dma((chunks, n_mem)), dma((chunks, n_mem)), dma((chunks, n_mem)),
            dma((n_lev,)), dma((n_lev,)), dma((chunks, n_lev)), dma((chunks, n_lev)),
        ],
        compiler_params=pltpu.CompilerParams(
            collective_id=0, has_side_effects=True, vmem_limit_bytes=56 * 2**20
        ),
        name="exchange",
    )(index, index, control, ens, loc_blocks.reshape(4, 4, chunks, neigh, TILE, TILE), obs_weight, channel_level_mask, obs_precision)
    late = (chunks - KEEP) * n_mem
    out = pl.pallas_call(
        functools.partial(adjoint_kernel, chunks, neigh),
        out_shape=jax.ShapeDtypeStruct((rows, points), jnp.float32),
        in_specs=[smem, hbm, hbm, hbm],
        out_specs=hbm,
        scratch_shapes=[
            pltpu.VMEM((rows, points), jnp.float32),
            pltpu.VMEM(back.shape, jnp.bfloat16),
            pltpu.VMEM((late, neigh * TILE, TILE), jnp.bfloat16),
            dma, dma, dma((late,)), dma,
        ],
        compiler_params=pltpu.CompilerParams(vmem_limit_bytes=63 * 2**20),
        name="adjoint",
    )(index, part, back, loc.reshape(n_mem, chunks, neigh * TILE, TILE))
    return out.reshape(control_vec.shape)


def solution(mesh):
    return jax.shard_map(
        functools.partial(body, mesh.shape["mem"], mesh.shape["lev"]),
        mesh=mesh,
        in_specs=(
            P("mem", "lev", None),
            P(None, None, "lev", "mem"),
            P(),
            P(),
            P(None, "lev", None),
            P("lev", None),
            P(None, "mem"),
        ),
        out_specs=P("mem", "lev", None),
        check_vma=False,
    )
```

```python
import functools
import math

import jax
import jax.numpy as jnp
from jax import lax
from jax.experimental import pallas as pl
from jax.experimental.pallas import tpu as pltpu
from jax.sharding import PartitionSpec as P

MESH = pl.DeviceIdType.MESH
TILE = 128
PAD = 32
KEEP = 3
SLOTS = 104
WAYS = 16
UNROLL = 13


def exchange_kernel(
    geo, idx_ref, idx_vec, ctrl_hbm, ens_hbm, loc_hbm, obs_ref, mask_ref, prec_hbm, back_hbm, part_hbm,
    arrived0, arrived1, arrived2, sums, table_vec, table, table_sem, part_sem, prec_ref, prec_sem, ctrl32, ctrl, loc, ens, send, recv, bsend, opg, incg,
    ctrl_sem, loc_sem, ens_sem, own_sem, fsend, frecv, bsend_sem, brecv_sem, osend, orecv, isend, irecv,
):
    n_mem, n_lev, chunks, neigh, scale = geo
    arrived = (arrived0, arrived1, arrived2)
    me = lax.axis_index("mem")
    lev = lax.axis_index("lev")
    my_x, my_z, my_c = lax.div(me, 4), lax.rem(lax.div(me, 2), 2), lax.rem(me, 2)
    rows = ctrl32.shape[0]
    per_dev = rows * 3
    groups = ctrl_sem.shape[0]
    span = ctrl32.shape[1] // groups

    def zc_of(g):
        return lax.rem(my_z + 1 - lax.div(g, 2), 2) * 2 + lax.rem(my_c + 1 - lax.rem(g, 2), 2)

    def peer(i):
        return lax.rem(my_x + 3 - lax.rem(i, 4), 4) * 4 + zc_of(lax.div(i, 4))

    def source(i):
        return lax.rem(my_x + 1 + lax.rem(i, 4), 4) * 4 + zc_of(lax.div(i, 4))

    def level_peer(j):
        return {"lev": lax.rem(lev + j, n_lev)}

    def ctrl_copy(g):
        cols = pl.ds(pl.multiple_of(g * span, TILE), span)
        return pltpu.make_async_copy(ctrl_hbm.at[:, cols], ctrl32.at[:, cols], ctrl_sem.at[g])

    def loc_copy(n):
        c, zc = lax.div(n, 4), zc_of(lax.rem(n, 4))
        return pltpu.make_async_copy(loc_hbm.at[:, zc, c], loc.at[c, zc], loc_sem.at[n])

    def repeat(lo, hi, fn):
        def step(n, carry):
            fn(n)
            return carry

        lax.fori_loop(lo, hi, step, 0)

    repeat(0, groups, lambda g: ctrl_copy(g).start())
    loc_copy(0).start()
    barrier = pltpu.get_barrier_semaphore()
    for i in range(n_mem - 1):
        pl.semaphore_signal(barrier, inc=1, device_id={"mem": peer(i)}, device_id_type=MESH)
    for j in range(1, n_lev):
        pl.semaphore_signal(barrier, inc=1, device_id=level_peer(j), device_id_type=MESH)
    ens_copy = pltpu.make_async_copy(ens_hbm, ens, ens_sem)
    prec_copy = pltpu.make_async_copy(prec_hbm, prec_ref, prec_sem)

    op = obs_ref[...].astype(jnp.float32) * mask_ref[...].astype(jnp.float32)[None]
    op = op.reshape(24, op.shape[2])
    op = jnp.concatenate([op, jnp.zeros((PAD - 24, op.shape[1]), jnp.float32)], axis=0)
    mine = pl.ds(pl.multiple_of(lev * PAD, PAD), PAD)
    opg[mine, :] = op.astype(jnp.bfloat16)

    per_group = span // TILE

    def convert(g):
        ctrl_copy(g).wait()
        loc_copy(g + 1).start()
        for u in range(per_group):
            s = g * per_group + u
            cols = pl.ds(pl.multiple_of(s * TILE, TILE), TILE)
            ctrl[s] = ctrl32[:, cols].astype(jnp.bfloat16)

    repeat(0, groups, convert)

    def tabulate(c):
        target = lax.broadcasted_iota(jnp.int32, (64, 64), 0)
        idx = idx_vec[...]
        hits = jnp.zeros((64, 64), jnp.int32)
        for k in range(neigh):
            hits = hits + jnp.where(target == idx[k : k + 1, :], k + 1, 0)
        hits = jnp.minimum(hits, neigh)
        lane = lax.broadcasted_iota(jnp.int32, (64, TILE), 1)

        def column(d):
            at = d * chunks + c
            return jnp.broadcast_to(hits[:, at : at + 1], (64, TILE))

        count = jnp.zeros((64, TILE), jnp.int32)
        for d in range(n_mem):
            count = count + jnp.minimum(column(d), 1)
        pairs = lax.div(count + 1, 2)
        slot = lane[:1]
        end = jnp.zeros((1, TILE), jnp.int32)
        base = jnp.zeros((1, TILE), jnp.int32)
        for s in range(64):
            table_vec[c, 8 + s : 9 + s] = end
            end = end + pairs[s : s + 1]
            base = jnp.where(end <= slot, end, base)
        begin = table_vec[c, 8:]
        even = jnp.zeros((64, TILE), jnp.int32)
        odd = jnp.zeros((64, TILE), jnp.int32)
        seen = jnp.zeros((64, TILE), jnp.int32)
        for d in range(n_mem):
            value = column(d)
            here = jnp.where((lane == begin + lax.div(seen, 2)) & (value > 0), value + d * WAYS, 0)
            second = lax.rem(seen, 2)
            even = even + here * (1 - second)
            odd = odd + here * second
            seen = seen + jnp.minimum(value, 1)

        def codes(values):
            for size in (32, 16, 8):
                values = values[:size] + values[size:]
            total = values[0:1]
            for s in range(1, 8):
                total = total + values[s : s + 1]
            return jnp.where(total > 0, total - 1, WAYS * n_mem)

        row = lax.broadcasted_iota(jnp.int32, (8, TILE), 0)
        head = jnp.where(row == 0, codes(even), jnp.where(row == 1, codes(odd), slot - base))
        table_vec[c, :8] = head
        last = jnp.maximum(begin + pairs - 1, 0)
        table_vec[c, 8:] = jnp.where(lane == 1, jnp.minimum(count, 1), last)
        arrived[c][n_mem] = jnp.zeros((rows, TILE), jnp.bfloat16)

    table_copy = pltpu.make_async_copy(table_vec, table, table_sem)

    def op_copy(j):
        return pltpu.make_async_remote_copy(
            src_ref=opg.at[mine], dst_ref=opg.at[mine], send_sem=osend.at[j], recv_sem=orecv.at[j],
            device_id=level_peer(j), device_id_type=MESH,
        )

    def inc_copy(c, j):
        return pltpu.make_async_remote_copy(
            src_ref=incg.at[c, mine], dst_ref=incg.at[c, mine],
            send_sem=isend.at[c, j], recv_sem=irecv.at[c, j],
            device_id=level_peer(j), device_id_type=MESH,
        )

    def fwd_copy(c, i):
        d = peer(i)
        return pltpu.make_async_remote_copy(
            src_ref=send.at[c, d], dst_ref=recv.at[c, me], send_sem=fsend.at[c, i], recv_sem=frecv.at[c, i],
            device_id={"mem": d}, device_id_type=MESH,
        )

    def landing(c):
        return arrived[c].at[me] if c < KEEP else back_hbm.at[c - KEEP, me]

    def bwd_copy(c, i):
        d = peer(i)
        return pltpu.make_async_remote_copy(
            src_ref=bsend.at[c, d], dst_ref=landing(c), send_sem=bsend_sem.at[c, i],
            recv_sem=brecv_sem.at[c, i], device_id={"mem": d}, device_id_type=MESH,
        )

    def localize(n):
        c, zc = lax.div(n, 4), zc_of(lax.rem(n, 4))
        loc_copy(n).wait()
        for u in range(4):
            x = lax.rem(my_x + 3 - u, 4)
            d = x * 4 + zc
            t = d * chunks + c
            picked = jnp.concatenate([ctrl[idx_ref[k, t]] for k in range(neigh)], axis=1)
            out = jnp.dot(picked, loc[c, zc, x].reshape(neigh * TILE, TILE), preferred_element_type=jnp.float32)
            send[c, d] = out.astype(jnp.bfloat16)

    def part(c, values, src, acc):
        cols = pl.ds(c * TILE, TILE)
        weights = values[c, src].astype(jnp.float32).reshape(rows // 8, 1, 8, TILE)
        pert = ens[pl.ds(pl.multiple_of(src * per_dev, per_dev), per_dev), cols]
        pert = pert.astype(jnp.float32).reshape(rows // 8, 3, 8, TILE)
        return acc + jnp.sum(pert * weights, axis=0)

    def increment(c):
        acc = part(c, send, me, jnp.zeros((3, 8, TILE), jnp.float32))

        def step(i, acc):
            fwd_copy(c, i).wait_recv()
            return part(c, recv, source(i), acc)

        acc = lax.fori_loop(0, n_mem - 1, step, acc) * scale
        acc = jnp.concatenate([acc.reshape(24, TILE), jnp.zeros((PAD - 24, TILE), jnp.float32)], axis=0)
        incg[c, mine, :] = acc.astype(jnp.bfloat16)
        repeat(1, n_lev, lambda j: inc_copy(c, j).start())

    def observe(c):
        repeat(1, n_lev, lambda j: inc_copy(c, j).wait_recv())
        cols = pl.ds(c * TILE, TILE)
        evolved = lax.dot_general(
            opg[...], incg[c], (((0,), (0,)), ((), ())), preferred_element_type=jnp.float32
        )
        weighted = (prec_ref[:, cols] * evolved).astype(jnp.bfloat16)
        grad = jnp.dot(opg[mine, :], weighted, preferred_element_type=jnp.float32)
        grad = grad.astype(jnp.bfloat16).astype(jnp.float32)[:24].reshape(1, 3, 8, TILE)

        def back(d):
            pert = ens[pl.ds(pl.multiple_of(d * per_dev, per_dev), per_dev), cols]
            pert = pert.astype(jnp.float32).reshape(rows // 8, 3, 8, TILE)
            out = jnp.sum(pert * grad, axis=1) * scale
            bsend[c, d] = out.reshape(rows, TILE).astype(jnp.bfloat16)

        repeat(0, n_mem, back)

    half = n_mem // 2

    def send_fwd(c, lo=0, hi=n_mem - 1):
        repeat(lo, hi, lambda i: fwd_copy(c, i).start())

    def own_copy(c):
        return pltpu.make_async_copy(bsend.at[c, me], landing(c), own_sem.at[c])

    def send_bwd(c, lo=0, hi=n_mem - 1):
        repeat(lo, hi, lambda i: bwd_copy(c, i).start())
        if lo == 0:
            own_copy(c).start()

    def first(n):
        loc_copy(n + groups + 1).start()
        localize(n)

    def send_group(n):
        c, g = lax.div(n, 4), lax.rem(n, 4)
        for u in range(4):
            if u < 3:
                fwd_copy(c, g * 4 + u).start()
            else:
                pl.when(g < 3)(lambda: fwd_copy(c, g * 4 + 3).start())

    def first_sent(n):
        first(n)
        send_group(n)

    def later_sent(n):
        localize(n)
        send_group(n)

    def part_copy(g):
        cols = pl.ds(pl.multiple_of(g * span, TILE), span)
        return pltpu.make_async_copy(ctrl32.at[:, cols], part_hbm.at[:, cols], part_sem.at[g])

    def gather(c):
        own_copy(c).wait()
        repeat(0, n_mem - 1, lambda i: bwd_copy(c, i).wait_recv())

        def block(code):
            d, k = lax.div(code, WAYS), lax.rem(code, WAYS)
            x, zc = lax.rem(lax.div(d, 4), 4), lax.rem(d, 4)
            return arrived[c][d], loc[c, zc, x, k]

        def slots(q, before):
            for u in range(UNROLL):
                p = q * UNROLL + u
                left, right = zip(block(table[c, 0, p]), block(table[c, 1, p]))
                value = lax.dot_general(
                    jnp.concatenate(left, axis=1), jnp.concatenate(right, axis=1), (((1,), (1,)), ((), ())),
                    preferred_element_type=jnp.float32,
                )
                before = value + jnp.minimum(table[c, 2, p], 1).astype(jnp.float32) * before
                sums[p] = before
            return before

        lax.fori_loop(0, SLOTS // UNROLL, slots, jnp.zeros((rows, TILE), jnp.float32))

        def settle(g):
            for u in range(per_group):
                s = g * per_group + u
                cols = pl.ds(pl.multiple_of(s * TILE, TILE), TILE)
                present = table[c, 8 + s, 1].astype(jnp.float32)
                ctrl32[:, cols] += present * sums[table[c, 8 + s, 0]]
            if c == KEEP - 1:
                part_copy(g).start()

        repeat(0, groups, settle)

    first(0)
    pl.semaphore_wait(barrier, n_mem - 1 + n_lev - 1)
    send_group(0)
    repeat(1, 4, first_sent)
    repeat(1, n_lev, lambda j: op_copy(j).start())
    repeat(4, chunks * 4 - groups - 1, first_sent)
    ens_copy.start()
    prec_copy.start()
    later_sent(chunks * 4 - groups - 1)
    repeat(8, 10, later_sent)
    repeat(10, 16, localize)
    ens_copy.wait()
    prec_copy.wait()
    increment(0)
    send_fwd(2, half)
    send_fwd(3, 0, half)
    increment(1)
    send_fwd(3, half)
    repeat(1, n_lev, lambda j: op_copy(j).wait())
    tabulate(0)
    tabulate(1)
    observe(0)
    send_bwd(0, 0, half)
    increment(2)
    send_bwd(0, half)
    observe(1)
    send_bwd(1, 0, half)
    tabulate(2)
    table_copy.start()
    increment(3)
    send_bwd(1, half)
    observe(2)
    send_bwd(2)
    table_copy.wait()
    gather(0)
    observe(3)
    send_bwd(3)
    for c in range(1, KEEP):
        gather(c)

    for c in range(chunks):
        if c >= KEEP:
            own_copy(c).wait()

        def finish(i):
            fwd_copy(c, i).wait_send()
            bwd_copy(c, i).wait_send()
            if c >= KEEP:
                bwd_copy(c, i).wait_recv()

        repeat(0, n_mem - 1, finish)
        repeat(1, n_lev, lambda j: inc_copy(c, j).wait_send())
    repeat(0, groups, lambda g: part_copy(g).wait())


def adjoint_kernel(
    chunks, neigh, idx_ref, part_hbm, back_hbm, loc_hbm, out_hbm, acc, part, back, loc, part_sem, back_sem, loc_sem, out_sem
):
    steps = loc_sem.shape[0]
    n_mem = back.shape[1]

    def loc_copy(n):
        return pltpu.make_async_copy(loc_hbm.at[n % n_mem, KEEP + n // n_mem], loc.at[n], loc_sem.at[n])

    back_copy = pltpu.make_async_copy(back_hbm, back, back_sem)
    part_copy = pltpu.make_async_copy(part_hbm, part, part_sem)
    back_copy.start()
    for n in range(steps):
        loc_copy(n).start()
    part_copy.start()
    acc[...] = jnp.zeros_like(acc)
    back_copy.wait()

    def group(g, carry):
        for u in range(4):
            loc_copy(g * 4 + u).wait()
        for u in range(4):
            n = g * 4 + u
            c, d = n // n_mem, n % n_mem
            t = d * chunks + c + KEEP
            vals = lax.dot_general(
                back[c, d], loc[n], (((1,), (1,)), ((), ())), preferred_element_type=jnp.float32
            )
            for k in range(neigh):
                cols = pl.ds(pl.multiple_of(idx_ref[k, t] * TILE, TILE), TILE)
                acc[:, cols] += vals[:, k * TILE : (k + 1) * TILE]
        return carry

    lax.fori_loop(0, steps // 4, group, 0)
    part_copy.wait()
    pieces = out_sem.shape[0]
    span = acc.shape[1] // pieces

    def out_copy(g):
        cols = pl.ds(pl.multiple_of(g * span, TILE), span)
        return pltpu.make_async_copy(acc.at[:, cols], out_hbm.at[:, cols], out_sem.at[g])

    def close(g, carry):
        cols = pl.ds(pl.multiple_of(g * span, TILE), span)
        acc[:, cols] += part[:, cols]
        out_copy(g).start()
        return carry

    def drain(g, carry):
        out_copy(g).wait()
        return carry

    lax.fori_loop(0, pieces, close, 0)
    lax.fori_loop(0, pieces, drain, 0)


def body(n_mem, n_lev, control_vec, ens_perturb, loc_blocks, tile_index, obs_weight, channel_level_mask, obs_precision):
    mem_rows, lev_rows, points = control_vec.shape
    members = ens_perturb.shape[0]
    tiles, neigh = tile_index.shape
    chunks = tiles // n_mem
    rows = mem_rows * lev_rows
    channels = obs_weight.shape[2]
    control = control_vec.reshape(rows, points)
    index = tile_index.T
    ens = ens_perturb.reshape(members * 3 * lev_rows, points // n_mem)
    loc = loc_blocks.reshape(tiles, neigh * TILE, TILE)
    hbm = pl.BlockSpec(memory_space=pltpu.HBM)
    vmem = pl.BlockSpec(memory_space=pltpu.VMEM)
    smem = pl.BlockSpec(memory_space=pltpu.SMEM)
    dma = pltpu.SemaphoreType.DMA
    geo = (n_mem, n_lev, chunks, neigh, 1.0 / math.sqrt(members - 1))
    wide = (chunks, n_mem, rows, TILE)
    back, part = pl.pallas_call(
        functools.partial(exchange_kernel, geo),
        out_shape=(
            jax.ShapeDtypeStruct((chunks - KEEP,) + wide[1:], jnp.bfloat16),
            jax.ShapeDtypeStruct((rows, points), jnp.float32),
        ),
        in_specs=[smem, vmem, hbm, hbm, hbm, vmem, vmem, hbm],
        out_specs=(hbm, hbm),
        scratch_shapes=[
            *[pltpu.VMEM((n_mem + 1, rows, TILE), jnp.bfloat16)] * KEEP,
            pltpu.VMEM((SLOTS, rows, TILE), jnp.float32),
            pltpu.VMEM((KEEP, 72, TILE), jnp.int32),
            pltpu.SMEM((KEEP, 72, TILE), jnp.int32),
            dma,
            dma((8,)),
            pltpu.VMEM(obs_precision.shape, jnp.float32),
            dma,
            pltpu.VMEM((rows, points), jnp.float32),
            pltpu.VMEM((tiles, rows, TILE), jnp.bfloat16),
            pltpu.VMEM((chunks, 4, 4, neigh, TILE, TILE), jnp.bfloat16),
            pltpu.VMEM(ens.shape, jnp.bfloat16),
            pltpu.VMEM(wide, jnp.bfloat16),
            pltpu.VMEM(wide, jnp.bfloat16),
            pltpu.VMEM(wide, jnp.bfloat16),
            pltpu.VMEM((n_lev * PAD, channels), jnp.bfloat16),
            pltpu.VMEM((chunks, n_lev * PAD, TILE), jnp.bfloat16),
            dma((8,)), dma((chunks * 4,)), dma, dma((chunks,)),
            dma((chunks, n_mem)), dma((chunks, n_mem)), dma((chunks, n_mem)), dma((chunks, n_mem)),
            dma((n_lev,)), dma((n_lev,)), dma((chunks, n_lev)), dma((chunks, n_lev)),
        ],
        compiler_params=pltpu.CompilerParams(
            collective_id=0, has_side_effects=True, vmem_limit_bytes=56 * 2**20
        ),
        name="exchange",
    )(index, index, control, ens, loc_blocks.reshape(4, 4, chunks, neigh, TILE, TILE), obs_weight, channel_level_mask, obs_precision)
    late = (chunks - KEEP) * n_mem
    out = pl.pallas_call(
        functools.partial(adjoint_kernel, chunks, neigh),
        out_shape=jax.ShapeDtypeStruct((rows, points), jnp.float32),
        in_specs=[smem, hbm, hbm, hbm],
        out_specs=hbm,
        scratch_shapes=[
            pltpu.VMEM((rows, points), jnp.float32),
            pltpu.VMEM((rows, points), jnp.float32),
            pltpu.VMEM(back.shape, jnp.bfloat16),
            pltpu.VMEM((late, neigh * TILE, TILE), jnp.bfloat16),
            dma, dma, dma((late,)), dma((8,)),
        ],
        compiler_params=pltpu.CompilerParams(vmem_limit_bytes=63 * 2**20),
        name="adjoint",
    )(index, part, back, loc.reshape(n_mem, chunks, neigh * TILE, TILE))
    return out.reshape(control_vec.shape)


def solution(mesh):
    return jax.shard_map(
        functools.partial(body, mesh.shape["mem"], mesh.shape["lev"]),
        mesh=mesh,
        in_specs=(
            P("mem", "lev", None),
            P(None, None, "lev", "mem"),
            P(),
            P(),
            P(None, "lev", None),
            P("lev", None),
            P(None, "mem"),
        ),
        out_specs=P("mem", "lev", None),
        check_vma=False,
    )
```

```python
import functools
import math

import jax
import jax.numpy as jnp
from jax import lax
from jax.experimental import pallas as pl
from jax.experimental.pallas import tpu as pltpu
from jax.sharding import PartitionSpec as P

MESH = pl.DeviceIdType.MESH
TILE = 128
PAD = 32
KEEP = 3
SLOTS = 104
WAYS = 16
UNROLL = 13


def exchange_kernel(
    geo, idx_ref, idx_vec, ctrl_hbm, ens_hbm, loc_hbm, obs_ref, mask_ref, prec_hbm, back_hbm, part_hbm,
    arrived0, arrived1, arrived2, sums, table_vec, table, table_sem, part_sem, prec_ref, prec_sem, ctrl32, ctrl, loc, ens, send, recv, bsend, opg, incg,
    ctrl_sem, loc_sem, ens_sem, own_sem, fsend, frecv, bsend_sem, brecv_sem, osend, orecv, isend, irecv,
):
    n_mem, n_lev, chunks, neigh, scale = geo
    arrived = (arrived0, arrived1, arrived2)
    me = lax.axis_index("mem")
    lev = lax.axis_index("lev")
    my_x, my_z, my_c = lax.div(me, 4), lax.rem(lax.div(me, 2), 2), lax.rem(me, 2)
    rows = ctrl32.shape[0]
    per_dev = rows * 3
    groups = ctrl_sem.shape[0]
    span = ctrl32.shape[1] // groups

    def zc_of(g):
        return lax.rem(my_z + 1 - lax.div(g, 2), 2) * 2 + lax.rem(my_c + 1 - lax.rem(g, 2), 2)

    def peer(i):
        return lax.rem(my_x + 3 - lax.rem(i, 4), 4) * 4 + zc_of(lax.div(i, 4))

    def source(i):
        return lax.rem(my_x + 1 + lax.rem(i, 4), 4) * 4 + zc_of(lax.div(i, 4))

    def level_peer(j):
        return {"lev": lax.rem(lev + j, n_lev)}

    def ctrl_copy(g):
        cols = pl.ds(pl.multiple_of(g * span, TILE), span)
        return pltpu.make_async_copy(ctrl_hbm.at[:, cols], ctrl32.at[:, cols], ctrl_sem.at[g])

    def loc_copy(n):
        c, zc = lax.div(n, 4), zc_of(lax.rem(n, 4))
        return pltpu.make_async_copy(loc_hbm.at[:, zc, c], loc.at[c, zc], loc_sem.at[n])

    def repeat(lo, hi, fn):
        def step(n, carry):
            fn(n)
            return carry

        lax.fori_loop(lo, hi, step, 0)

    repeat(0, groups, lambda g: ctrl_copy(g).start())
    loc_copy(0).start()
    barrier = pltpu.get_barrier_semaphore()
    for i in range(n_mem - 1):
        pl.semaphore_signal(barrier, inc=1, device_id={"mem": peer(i)}, device_id_type=MESH)
    for j in range(1, n_lev):
        pl.semaphore_signal(barrier, inc=1, device_id=level_peer(j), device_id_type=MESH)
    ens_copy = pltpu.make_async_copy(ens_hbm, ens, ens_sem)
    prec_copy = pltpu.make_async_copy(prec_hbm, prec_ref, prec_sem)

    op = obs_ref[...].astype(jnp.float32) * mask_ref[...].astype(jnp.float32)[None]
    op = op.reshape(24, op.shape[2])
    op = jnp.concatenate([op, jnp.zeros((PAD - 24, op.shape[1]), jnp.float32)], axis=0)
    mine = pl.ds(pl.multiple_of(lev * PAD, PAD), PAD)
    opg[mine, :] = op.astype(jnp.bfloat16)

    per_group = span // TILE

    def convert(g):
        ctrl_copy(g).wait()
        loc_copy(g + 1).start()
        for u in range(per_group):
            s = g * per_group + u
            cols = pl.ds(pl.multiple_of(s * TILE, TILE), TILE)
            ctrl[s] = ctrl32[:, cols].astype(jnp.bfloat16)

    repeat(0, groups, convert)

    def tabulate(c):
        target = lax.broadcasted_iota(jnp.int32, (64, 64), 0)
        idx = idx_vec[...]
        hits = jnp.zeros((64, 64), jnp.int32)
        for k in range(neigh):
            hits = hits + jnp.where(target == idx[k : k + 1, :], k + 1, 0)
        hits = jnp.minimum(hits, neigh)
        lane = lax.broadcasted_iota(jnp.int32, (64, TILE), 1)

        def column(d):
            at = d * chunks + c
            return jnp.broadcast_to(hits[:, at : at + 1], (64, TILE))

        count = jnp.zeros((64, TILE), jnp.int32)
        for d in range(n_mem):
            count = count + jnp.minimum(column(d), 1)
        pairs = lax.div(count + 1, 2)
        slot = lane[:1]
        end = jnp.zeros((1, TILE), jnp.int32)
        base = jnp.zeros((1, TILE), jnp.int32)
        for s in range(64):
            table_vec[c, 8 + s : 9 + s] = end
            end = end + pairs[s : s + 1]
            base = jnp.where(end <= slot, end, base)
        begin = table_vec[c, 8:]
        even = jnp.zeros((64, TILE), jnp.int32)
        odd = jnp.zeros((64, TILE), jnp.int32)
        seen = jnp.zeros((64, TILE), jnp.int32)
        for d in range(n_mem):
            value = column(d)
            here = jnp.where((lane == begin + lax.div(seen, 2)) & (value > 0), value + d * WAYS, 0)
            second = lax.rem(seen, 2)
            even = even + here * (1 - second)
            odd = odd + here * second
            seen = seen + jnp.minimum(value, 1)

        def codes(values):
            for size in (32, 16, 8):
                values = values[:size] + values[size:]
            total = values[0:1]
            for s in range(1, 8):
                total = total + values[s : s + 1]
            return jnp.where(total > 0, total - 1, WAYS * n_mem)

        row = lax.broadcasted_iota(jnp.int32, (8, TILE), 0)
        head = jnp.where(row == 0, codes(even), jnp.where(row == 1, codes(odd), slot - base))
        table_vec[c, :8] = head
        last = jnp.maximum(begin + pairs - 1, 0)
        table_vec[c, 8:] = jnp.where(lane == 1, jnp.minimum(count, 1), last)
        arrived[c][n_mem] = jnp.zeros((rows, TILE), jnp.bfloat16)

    table_copy = pltpu.make_async_copy(table_vec, table, table_sem)

    def op_copy(j):
        return pltpu.make_async_remote_copy(
            src_ref=opg.at[mine], dst_ref=opg.at[mine], send_sem=osend.at[j], recv_sem=orecv.at[j],
            device_id=level_peer(j), device_id_type=MESH,
        )

    def inc_copy(c, j):
        return pltpu.make_async_remote_copy(
            src_ref=incg.at[c, mine], dst_ref=incg.at[c, mine],
            send_sem=isend.at[c, j], recv_sem=irecv.at[c, j],
            device_id=level_peer(j), device_id_type=MESH,
        )

    def fwd_copy(c, i):
        d = peer(i)
        return pltpu.make_async_remote_copy(
            src_ref=send.at[c, d], dst_ref=recv.at[c, me], send_sem=fsend.at[c, i], recv_sem=frecv.at[c, i],
            device_id={"mem": d}, device_id_type=MESH,
        )

    def landing(c):
        return arrived[c].at[me] if c < KEEP else back_hbm.at[c - KEEP, me]

    def bwd_copy(c, i):
        d = peer(i)
        return pltpu.make_async_remote_copy(
            src_ref=bsend.at[c, d], dst_ref=landing(c), send_sem=bsend_sem.at[c, i],
            recv_sem=brecv_sem.at[c, i], device_id={"mem": d}, device_id_type=MESH,
        )

    def localize(n):
        c, zc = lax.div(n, 4), zc_of(lax.rem(n, 4))
        loc_copy(n).wait()
        for u in range(4):
            x = lax.rem(my_x + 3 - u, 4)
            d = x * 4 + zc
            t = d * chunks + c
            picked = jnp.concatenate([ctrl[idx_ref[k, t]] for k in range(neigh)], axis=1)
            out = jnp.dot(picked, loc[c, zc, x].reshape(neigh * TILE, TILE), preferred_element_type=jnp.float32)
            send[c, d] = out.astype(jnp.bfloat16)

    def part(c, values, src, acc):
        cols = pl.ds(c * TILE, TILE)
        weights = values[c, src].astype(jnp.float32).reshape(rows // 8, 1, 8, TILE)
        pert = ens[pl.ds(pl.multiple_of(src * per_dev, per_dev), per_dev), cols]
        pert = pert.astype(jnp.float32).reshape(rows // 8, 3, 8, TILE)
        return acc + jnp.sum(pert * weights, axis=0)

    def increment(c):
        acc = part(c, send, me, jnp.zeros((3, 8, TILE), jnp.float32))

        def step(i, acc):
            fwd_copy(c, i).wait_recv()
            return part(c, recv, source(i), acc)

        acc = lax.fori_loop(0, n_mem - 1, step, acc) * scale
        acc = jnp.concatenate([acc.reshape(24, TILE), jnp.zeros((PAD - 24, TILE), jnp.float32)], axis=0)
        incg[c, mine, :] = acc.astype(jnp.bfloat16)
        repeat(1, n_lev, lambda j: inc_copy(c, j).start())

    def observe(c):
        repeat(1, n_lev, lambda j: inc_copy(c, j).wait_recv())
        cols = pl.ds(c * TILE, TILE)
        evolved = lax.dot_general(
            opg[...], incg[c], (((0,), (0,)), ((), ())), preferred_element_type=jnp.float32
        )
        weighted = (prec_ref[:, cols] * evolved).astype(jnp.bfloat16)
        grad = jnp.dot(opg[mine, :], weighted, preferred_element_type=jnp.float32)
        grad = grad.astype(jnp.bfloat16).astype(jnp.float32)[:24].reshape(1, 3, 8, TILE)

        def back(d):
            pert = ens[pl.ds(pl.multiple_of(d * per_dev, per_dev), per_dev), cols]
            pert = pert.astype(jnp.float32).reshape(rows // 8, 3, 8, TILE)
            out = jnp.sum(pert * grad, axis=1) * scale
            bsend[c, d] = out.reshape(rows, TILE).astype(jnp.bfloat16)

        repeat(0, n_mem, back)

    half = n_mem // 2

    def send_fwd(c, lo=0, hi=n_mem - 1):
        repeat(lo, hi, lambda i: fwd_copy(c, i).start())

    def own_copy(c):
        return pltpu.make_async_copy(bsend.at[c, me], landing(c), own_sem.at[c])

    def send_bwd(c, lo=0, hi=n_mem - 1):
        repeat(lo, hi, lambda i: bwd_copy(c, i).start())
        if lo == 0:
            own_copy(c).start()

    def first(n):
        loc_copy(n + groups + 1).start()
        localize(n)

    def send_group(n):
        c, g = lax.div(n, 4), lax.rem(n, 4)
        for u in range(4):
            if u < 3:
                fwd_copy(c, g * 4 + u).start()
            else:
                pl.when(g < 3)(lambda: fwd_copy(c, g * 4 + 3).start())

    def first_sent(n):
        first(n)
        send_group(n)

    def later_sent(n):
        localize(n)
        send_group(n)

    def part_copy(g):
        cols = pl.ds(pl.multiple_of(g * span, TILE), span)
        return pltpu.make_async_copy(ctrl32.at[:, cols], part_hbm.at[:, cols], part_sem.at[g])

    def gather(c):
        own_copy(c).wait()
        repeat(0, n_mem - 1, lambda i: bwd_copy(c, i).wait_recv())

        def block(code):
            d, k = lax.div(code, WAYS), lax.rem(code, WAYS)
            x, zc = lax.rem(lax.div(d, 4), 4), lax.rem(d, 4)
            return arrived[c][d], loc[c, zc, x, k]

        def slots(q, before):
            for u in range(UNROLL):
                p = q * UNROLL + u
                left, right = zip(block(table[c, 0, p]), block(table[c, 1, p]))
                value = lax.dot_general(
                    jnp.concatenate(left, axis=1), jnp.concatenate(right, axis=1), (((1,), (1,)), ((), ())),
                    preferred_element_type=jnp.float32,
                )
                before = value + jnp.minimum(table[c, 2, p], 1).astype(jnp.float32) * before
                sums[p] = before
            return before

        lax.fori_loop(0, SLOTS // UNROLL, slots, jnp.zeros((rows, TILE), jnp.float32))

        def settle(g):
            for u in range(per_group):
                s = g * per_group + u
                cols = pl.ds(pl.multiple_of(s * TILE, TILE), TILE)
                present = table[c, 8 + s, 1].astype(jnp.float32)
                ctrl32[:, cols] += present * sums[table[c, 8 + s, 0]]
            if c == KEEP - 1:
                part_copy(g).start()

        repeat(0, groups, settle)

    first(0)
    pl.semaphore_wait(barrier, n_mem - 1 + n_lev - 1)
    send_group(0)
    repeat(1, 4, first_sent)
    repeat(1, n_lev, lambda j: op_copy(j).start())
    repeat(4, chunks * 4 - groups - 1, first_sent)
    ens_copy.start()
    prec_copy.start()
    later_sent(chunks * 4 - groups - 1)
    repeat(8, 10, later_sent)
    repeat(10, 16, localize)
    ens_copy.wait()
    prec_copy.wait()
    increment(0)
    send_fwd(2, half)
    send_fwd(3, 0, half)
    increment(1)
    send_fwd(3, half)
    repeat(1, n_lev, lambda j: op_copy(j).wait())
    tabulate(0)
    tabulate(1)
    observe(0)
    send_bwd(0, 0, half)
    increment(2)
    send_bwd(0, half)
    observe(1)
    send_bwd(1, 0, half)
    tabulate(2)
    table_copy.start()
    increment(3)
    send_bwd(1, half)
    observe(2)
    send_bwd(2)
    table_copy.wait()
    gather(0)
    observe(3)
    send_bwd(3)
    for c in range(1, KEEP):
        gather(c)

    for c in range(chunks):
        if c >= KEEP:
            own_copy(c).wait()

        def finish(i):
            fwd_copy(c, i).wait_send()
            bwd_copy(c, i).wait_send()
            if c >= KEEP:
                bwd_copy(c, i).wait_recv()

        repeat(0, n_mem - 1, finish)
        repeat(1, n_lev, lambda j: inc_copy(c, j).wait_send())
    repeat(0, groups, lambda g: part_copy(g).wait())


def adjoint_kernel(
    chunks, neigh, idx_ref, part_hbm, back_hbm, loc_hbm, out_hbm, acc, part, back, loc, part_sem, back_sem, loc_sem, out_sem
):
    steps = loc_sem.shape[0]
    n_mem = back.shape[1]

    def loc_copy(n):
        return pltpu.make_async_copy(loc_hbm.at[n % n_mem, KEEP + n // n_mem], loc.at[n], loc_sem.at[n])

    back_copy = pltpu.make_async_copy(back_hbm, back, back_sem)
    part_copy = pltpu.make_async_copy(part_hbm, part, part_sem)
    back_copy.start()
    for n in range(8):
        loc_copy(n).start()
    acc[...] = jnp.zeros_like(acc)
    back_copy.wait()

    def group(g, carry):
        for u in range(4):
            loc_copy(g * 4 + u).wait()

        @pl.when(g + 2 < steps // 4)
        def _():
            for u in range(4):
                loc_copy(g * 4 + 8 + u).start()

        @pl.when(g == 1)
        def _():
            part_copy.start()

        for u in range(4):
            n = g * 4 + u
            c, d = n // n_mem, n % n_mem
            t = d * chunks + c + KEEP
            vals = lax.dot_general(
                back[c, d], loc[n], (((1,), (1,)), ((), ())), preferred_element_type=jnp.float32
            )
            for k in range(neigh):
                cols = pl.ds(pl.multiple_of(idx_ref[k, t] * TILE, TILE), TILE)
                acc[:, cols] += vals[:, k * TILE : (k + 1) * TILE]
        return carry

    lax.fori_loop(0, steps // 4, group, 0)
    part_copy.wait()
    pieces = out_sem.shape[0]
    span = acc.shape[1] // pieces

    def out_copy(g):
        cols = pl.ds(pl.multiple_of(g * span, TILE), span)
        return pltpu.make_async_copy(acc.at[:, cols], out_hbm.at[:, cols], out_sem.at[g])

    def close(g, carry):
        cols = pl.ds(pl.multiple_of(g * span, TILE), span)
        acc[:, cols] += part[:, cols]
        out_copy(g).start()
        return carry

    def drain(g, carry):
        out_copy(g).wait()
        return carry

    lax.fori_loop(0, pieces, close, 0)
    lax.fori_loop(0, pieces, drain, 0)


def body(n_mem, n_lev, control_vec, ens_perturb, loc_blocks, tile_index, obs_weight, channel_level_mask, obs_precision):
    mem_rows, lev_rows, points = control_vec.shape
    members = ens_perturb.shape[0]
    tiles, neigh = tile_index.shape
    chunks = tiles // n_mem
    rows = mem_rows * lev_rows
    channels = obs_weight.shape[2]
    control = control_vec.reshape(rows, points)
    index = tile_index.T
    ens = ens_perturb.reshape(members * 3 * lev_rows, points // n_mem)
    loc = loc_blocks.reshape(tiles, neigh * TILE, TILE)
    hbm = pl.BlockSpec(memory_space=pltpu.HBM)
    vmem = pl.BlockSpec(memory_space=pltpu.VMEM)
    smem = pl.BlockSpec(memory_space=pltpu.SMEM)
    dma = pltpu.SemaphoreType.DMA
    geo = (n_mem, n_lev, chunks, neigh, 1.0 / math.sqrt(members - 1))
    wide = (chunks, n_mem, rows, TILE)
    back, part = pl.pallas_call(
        functools.partial(exchange_kernel, geo),
        out_shape=(
            jax.ShapeDtypeStruct((chunks - KEEP,) + wide[1:], jnp.bfloat16),
            jax.ShapeDtypeStruct((rows, points), jnp.float32),
        ),
        in_specs=[smem, vmem, hbm, hbm, hbm, vmem, vmem, hbm],
        out_specs=(hbm, hbm),
        scratch_shapes=[
            *[pltpu.VMEM((n_mem + 1, rows, TILE), jnp.bfloat16)] * KEEP,
            pltpu.VMEM((SLOTS, rows, TILE), jnp.float32),
            pltpu.VMEM((KEEP, 72, TILE), jnp.int32),
            pltpu.SMEM((KEEP, 72, TILE), jnp.int32),
            dma,
            dma((8,)),
            pltpu.VMEM(obs_precision.shape, jnp.float32),
            dma,
            pltpu.VMEM((rows, points), jnp.float32),
            pltpu.VMEM((tiles, rows, TILE), jnp.bfloat16),
            pltpu.VMEM((chunks, 4, 4, neigh, TILE, TILE), jnp.bfloat16),
            pltpu.VMEM(ens.shape, jnp.bfloat16),
            pltpu.VMEM(wide, jnp.bfloat16),
            pltpu.VMEM(wide, jnp.bfloat16),
            pltpu.VMEM(wide, jnp.bfloat16),
            pltpu.VMEM((n_lev * PAD, channels), jnp.bfloat16),
            pltpu.VMEM((chunks, n_lev * PAD, TILE), jnp.bfloat16),
            dma((8,)), dma((chunks * 4,)), dma, dma((chunks,)),
            dma((chunks, n_mem)), dma((chunks, n_mem)), dma((chunks, n_mem)), dma((chunks, n_mem)),
            dma((n_lev,)), dma((n_lev,)), dma((chunks, n_lev)), dma((chunks, n_lev)),
        ],
        compiler_params=pltpu.CompilerParams(
            collective_id=0, has_side_effects=True, vmem_limit_bytes=56 * 2**20
        ),
        name="exchange",
    )(index, index, control, ens, loc_blocks.reshape(4, 4, chunks, neigh, TILE, TILE), obs_weight, channel_level_mask, obs_precision)
    late = (chunks - KEEP) * n_mem
    out = pl.pallas_call(
        functools.partial(adjoint_kernel, chunks, neigh),
        out_shape=jax.ShapeDtypeStruct((rows, points), jnp.float32),
        in_specs=[smem, hbm, hbm, hbm],
        out_specs=hbm,
        scratch_shapes=[
            pltpu.VMEM((rows, points), jnp.float32),
            pltpu.VMEM((rows, points), jnp.float32),
            pltpu.VMEM(back.shape, jnp.bfloat16),
            pltpu.VMEM((late, neigh * TILE, TILE), jnp.bfloat16),
            dma, dma, dma((late,)), dma((8,)),
        ],
        compiler_params=pltpu.CompilerParams(vmem_limit_bytes=63 * 2**20),
        name="adjoint",
    )(index, part, back, loc.reshape(n_mem, chunks, neigh * TILE, TILE))
    return out.reshape(control_vec.shape)


def solution(mesh):
    return jax.shard_map(
        functools.partial(body, mesh.shape["mem"], mesh.shape["lev"]),
        mesh=mesh,
        in_specs=(
            P("mem", "lev", None),
            P(None, None, "lev", "mem"),
            P(),
            P(),
            P(None, "lev", None),
            P("lev", None),
            P(None, "mem"),
        ),
        out_specs=P("mem", "lev", None),
        check_vma=False,
    )
```
